256 devices in a mesh: rows: 64 (over z, y, core), cols: 4 (over x).
Axes of the slice: x: 4, y: 4, z: 8, core: 2. Of those that a mesh axis runs over, the one named last changes fastest.
Arguments:
- cotangent: float32 [65536, 2048], P('rows', 'cols'), may hold values from -6 to 6
- saved: float32 [65536, 2048], P('rows', 'cols'), may hold values from -0.125 to 0.125
- panel: float32 [1024, 65536], P(None, 'rows'), may hold values from -0.25 to 0.25
- dinv: float32 [2, 512, 512], replicated, as said below
Outputs:
- cotangent_out: float32 [65536, 2048], P('rows', 'cols')
- factor_grad: float32 [2, 512, 65536], P(None, 'cols', 'rows')
The draws below stay inside these ranges and needn't reach their ends.
Inputs may be any that keep to these rules, and one draw needn't show every extreme that they name: Each dinv[k] is lower triangular with a positive diagonal.
All inputs are finite; a program needn't handle non-finite values.
Results may differ from the reference program's by a relative error of at most 0.0001.
Values sent between devices are 32-bit elements; how exact they have to be, the bound alone decides.
No kernel may reach another device: no remote copies, remote signals or barrier semaphores. Data moves between devices by JAX's collectives and lax.ppermute only.
A program may use at most 64 MiB of HBM per device.

```python
import math
import jax
import jax.numpy as jnp
from jax import lax

N = 65536
BS = 512
STEPS = 2
R = 2048


def draw_dinv(key, part):
    key = jax.random.fold_in(key, 7)
    key_diag, key_lower = jax.random.split(key)
    diagonal_vals = jnp.exp(jax.random.uniform(key_diag, (STEPS, BS), jnp.float32, math.log(0.5), math.log(2.0)))
    lower_vals = jnp.clip(jax.random.normal(key_lower, (STEPS, BS, BS), jnp.float32), -6.0, 6.0)
    row_index = lax.broadcasted_iota(jnp.int32, (BS, BS), 0)
    column_index = lax.broadcasted_iota(jnp.int32, (BS, BS), 1)
    below_diag = (column_index < row_index).astype(jnp.float32)
    on_diag = column_index == row_index
    result = lower_vals * (0.8 / math.sqrt(BS)) * below_diag + jnp.where(on_diag, diagonal_vals[:, :, None], 0.0)
    return result.astype(jnp.float32)


def block_scale(rng, shape, cuts, smallest, high):
    level = 1.0
    for axis_at, shards_of in cuts:
        steps = jax.random.uniform(jax.random.fold_in(jax.random.fold_in(rng, 6), axis_at), (shards_of,), jnp.float32, smallest / len(cuts), high / len(cuts))
        level = level * jnp.repeat(jnp.exp(steps), shape[axis_at] // shards_of).reshape((-1,) + (1,) * (len(shape) - 1 - axis_at))
    return level


def bell_draw(key, shape, deviation, reach, pieces=(), held_as=jnp.bfloat16):
    values = jax.random.normal(key, shape, jnp.float32) * deviation
    if len(pieces) > 0:
        values = block_scale(key, shape, pieces, -0.22, 0.18) * values
    return jnp.clip(values, min=-reach, max=reach).astype(held_as)


def setup_inputs(seed: int = 0) -> dict:
    arg_keys = jax.random.split(jax.random.key(seed), 5)
    cotangent = bell_draw(arg_keys[0], (N, R), 1.0, 6.0, ((0, 64), (1, 4)), jnp.float32)
    saved = bell_draw(arg_keys[1], (N, R), R ** -0.5, 0.125, ((0, 64), (1, 4)), jnp.float32)
    panel = bell_draw(arg_keys[2], (STEPS * BS, N), BS ** -0.5, 0.25, ((1, 64),), jnp.float32)
    dinv = draw_dinv(jax.random.fold_in(arg_keys[4], 71), 0)
    return {"cotangent": cotangent, "saved": saved, "panel": panel, "dinv": dinv}


def reference(cotangent, saved, panel, dinv):
    carried = cotangent
    window_start = N - STEPS * BS
    row_index = jnp.arange(BS, dtype=jnp.int32)[:, None]
    column_index = jnp.arange(N, dtype=jnp.int32)[None, :]
    grad_list = [None] * STEPS
    for k in range(STEPS - 1, -1, -1):
        block_start = window_start + k * BS
        block_rows = carried[block_start:block_start + BS]
        solved = jnp.dot(dinv[k].T, block_rows, precision=lax.Precision.HIGHEST, preferred_element_type=jnp.float32)
        panel_rows = panel[k * BS:(k + 1) * BS, :block_start]
        update = jnp.dot(panel_rows.T, solved, precision=lax.Precision.HIGHEST, preferred_element_type=jnp.float32)
        carried = jnp.concatenate([carried[:block_start] - update, solved, carried[block_start + BS:]], 0)
        product = jnp.dot(solved, saved.T, precision=lax.Precision.HIGHEST, preferred_element_type=jnp.float32)
        grad_list[k] = jnp.where(column_index <= block_start + row_index, -product, jnp.float32(0.0))
    return carried, jnp.stack(grad_list, 0)
```

```python
import jax
import jax.numpy as jnp
from jax import lax
from jax.sharding import PartitionSpec as P

STEPS = 2
LEAD = (((0,), (0,)), ((), ()))
LAST = (((1,), (1,)), ((), ()))
NZ, NY, NX = 8, 4, 4
ROOT_Z, ROOT_Y = NZ - 1, NY - 1


def rank(z, y, c):
    return ((z % NZ) * NY + y % NY) * 2 + c


def carrier(z):
    return 0 if z in (4, 5, 6) else 1


ROOT = rank(ROOT_Z, ROOT_Y, 1)
SWAP = [(r, r ^ 1) for r in range(NZ * NY * 2)]
Y_SCATTER = [[(ROOT, rank(ROOT_Z, ROOT_Y + i, 1))] for i in range(1, NY)]
Z_SEND = [
    [(rank(ROOT_Z, y, 1), rank(ROOT_Z + d, y, 1)) for y in range(NY)]
    + [(rank(ROOT_Z, y, 0), rank(ROOT_Z - d, y, 0)) for y in range(NY) if d < 4]
    for d in (4, 3, 2, 1)
]
Y_SHIFT = [
    [(rank(z, y, carrier(z)), rank(z, y + s, carrier(z))) for z in range(NZ) for y in range(NY)]
    for s in range(1, NY)
]
X_RIGHT = [(q, (q + 1) % NX) for q in range(NX)]
X_LEFT = [(q, (q - 1) % NX) for q in range(NX)]


def dot(a, b, dims):
    return lax.dot_general(a, b, dims, precision=lax.Precision.HIGH, preferred_element_type=jnp.float32)


def on_device(cotangent, saved, panel, dinv):
    bs = dinv.shape[1]
    quarter = bs // 4
    half = quarter // 2
    me = lax.axis_index("rows")
    q = lax.axis_index("cols")
    z, y, c = me // (2 * NY), (me // 2) % NY, me % 2
    is_root = me == ROOT
    in_root_z = z == ROOT_Z
    is_carrier = c == jnp.where((z >= 4) & (z <= 6), 0, 1)
    mine = (y - ROOT_Y) % NY

    def rows(x, perm):
        return lax.ppermute(x, "rows", perm)

    def broadcast(x):
        parts = [x[i * quarter : (i + 1) * quarter] for i in range(4)]
        got = [rows(parts[i + 1], Y_SCATTER[i]) for i in range(3)]
        piece = jnp.where(is_root, parts[0], got[0] + got[1] + got[2])
        other = rows(piece, SWAP)
        piece = jnp.where(c == 1, piece, other)
        sent = [rows(piece, p) for p in Z_SEND]
        piece = jnp.where(in_root_z, piece, sent[0] + sent[1] + sent[2] + sent[3])
        back = [rows(piece, p) for p in Y_SHIFT]
        whole = jnp.concatenate([piece, back[2], back[1], back[0]], 0)
        other = rows(whole, SWAP)
        return jnp.where(is_carrier, whole, other)

    def turned(x, by):
        twice = jnp.concatenate([x, x], 0)
        return lax.dynamic_slice_in_dim(twice, by * quarter, bs, 0)

    def gradient(k, cyclic):
        from_q = turned(cyclic, (q - mine) % 4)
        a, b = quarter + half, 2 * quarter + half
        to_right = dot(from_q[a:b], saved, LAST)
        to_left = dot(from_q[b : b + quarter], saved, LAST)
        left1 = lax.ppermute(to_right, "cols", X_RIGHT)
        right1 = lax.ppermute(to_left, "cols", X_LEFT)
        next_a = dot(from_q[quarter:a], saved, LAST)
        prev_b = dot(from_q[b + quarter :], saved, LAST)
        own = dot(from_q[:quarter], saved, LAST)
        left2 = lax.ppermute(next_a + left1[half:], "cols", X_RIGHT)
        right2 = lax.ppermute(prev_b + right1[:half], "cols", X_LEFT)
        total = jnp.concatenate(
            [own[:half] + right1[half:] + left2, own[half:] + left1[:half] + right2], 0
        )
        first = me * cotangent.shape[0]
        start = NZ * NY * 2 * cotangent.shape[0] - STEPS * bs + k * bs
        limit = start + q * quarter + lax.broadcasted_iota(jnp.int32, (quarter, 1), 0)
        column = first + lax.broadcasted_iota(jnp.int32, (1, cotangent.shape[0]), 1)
        return jnp.where(column <= limit, -total, jnp.float32(0.0))

    local1 = dot(dinv[1], cotangent[bs:], LEAD)
    cyclic1 = broadcast(local1)
    local0 = dot(dinv[0], cotangent[:bs] - dot(panel[bs:, :bs], local1, LEAD), LEAD)
    cyclic0 = broadcast(local0)
    grad1 = gradient(1, cyclic1)
    grad0 = gradient(0, cyclic0)
    update = dot(panel[bs:], turned(cyclic1, (-mine) % 4), LEAD)
    update += dot(panel[:bs], turned(cyclic0, (-mine) % 4), LEAD)
    carried = jnp.where(is_root, jnp.concatenate([local0, local1], 0), cotangent - update)
    return carried, jnp.stack([grad0, grad1], 0)


def solution(mesh):
    return jax.shard_map(
        on_device,
        mesh=mesh,
        in_specs=(P("rows", "cols"), P("rows", "cols"), P(None, "rows"), P()),
        out_specs=(P("rows", "cols"), P(None, "cols", "rows")),
        check_vma=False,
    )
```

```python
import jax
import jax.numpy as jnp
from jax import lax
from jax.experimental import pallas as pl
from jax.experimental.pallas import tpu as pltpu
from jax.sharding import PartitionSpec as P

STEPS = 2
LEAD = (((0,), (0,)), ((), ()))
LAST = (((1,), (1,)), ((), ()))
NZ, NY, NX = 8, 4, 4
CHIPS = NZ * NY
ROOT = 2 * CHIPS - 1
VMEM_LIMIT = 48 * 1024 * 1024


def rank(z, y, c):
    return (z * NY + y) * 2 + c


SWAP = [(r, r ^ 1) for r in range(2 * CHIPS)]
ALONG_Y = [[rank(z, y, c) for y in range(NY)] for z in range(NZ) for c in range(2)]
ALONG_Z = [[rank(z, y, c) for z in range(NZ)] for y in range(NY) for c in range(2)]
X_RIGHT = [(q, (q + 1) % NX) for q in range(NX)]
X_LEFT = [(q, (q - 1) % NX) for q in range(NX)]


def split(x):
    high = x.astype(jnp.bfloat16)
    return high, (x - high.astype(jnp.float32)).astype(jnp.bfloat16)


def dot3(a, b, dims):
    def one(x, y):
        return lax.dot_general(x, y, dims, preferred_element_type=jnp.float32)

    return one(a[0], b[0]) + (one(a[0], b[1]) + one(a[1], b[0]))


def solve_kernel(cot_ref, panel_ref, dinv_ref, *out_refs):
    bs = dinv_ref.shape[1]
    half = bs // 8

    def put(k, solved):
        for quarter in range(4):
            for h in range(2):
                row = (quarter * 2 + h) * half
                out_refs[h][quarter, k] = solved[row : row + half]

    solved1 = dot3(split(dinv_ref[1]), split(cot_ref[bs:]), LEAD)
    put(1, solved1)
    left = cot_ref[:bs] - dot3(split(panel_ref[...]), split(solved1), LEAD)
    put(0, dot3(split(dinv_ref[0]), split(left), LEAD))


def solve(cotangent, panel, dinv):
    steps, bs, _ = dinv.shape
    rows, cols = cotangent.shape
    return pl.pallas_call(
        solve_kernel,
        grid=(1,),
        in_specs=[
            pl.BlockSpec((rows, cols), lambda i: (0, 0)),
            pl.BlockSpec((bs, bs), lambda i: (1, 0)),
            pl.BlockSpec((steps, bs, bs), lambda i: (0, 0, 0)),
        ],
        out_specs=[pl.BlockSpec((4, steps, bs // 8, cols), lambda i: (0, 0, 0, 0))] * 2,
        out_shape=[jax.ShapeDtypeStruct((4, steps, bs // 8, cols), jnp.float32)] * 2,
        compiler_params=pltpu.CompilerParams(vmem_limit_bytes=VMEM_LIMIT),
        cost_estimate=pl.CostEstimate(flops=18 * bs * bs * cols, bytes_accessed=7 << 20, transcendentals=0),
    )(cotangent, panel, dinv)


def update_kernel(at_ref, cot_ref, panel_ref, mine_ref, other_ref, out_ref, whole, high, low):
    i = pl.program_id(0)
    half = mine_ref.shape[2]
    tile = out_ref.shape[0]
    core = at_ref[2]

    @pl.when(i == 0)
    def _():
        for k in range(STEPS):
            for quarter in range(4):
                a, b = mine_ref[quarter, k], other_ref[quarter, k]
                for h in range(2):
                    rows = jnp.where(core == h, a, b)
                    at = pl.ds(((k * 4 + quarter) * 2 + h) * half, half)
                    whole[at, :] = rows
                    high[at, :], low[at, :] = split(rows)

    @pl.when(at_ref[0] != ROOT)
    def _():
        product = dot3(split(panel_ref[...]), (high[...], low[...]), LEAD)
        out_ref[...] = cot_ref[...] - product

    @pl.when(at_ref[0] == ROOT)
    def _():
        out_ref[...] = whole[pl.ds(pl.multiple_of(i * tile, tile), tile), :]


def update(at, cotangent, panel, mine, other):
    rows, cols = cotangent.shape
    tile = rows // 4
    halves = pl.BlockSpec(mine.shape, lambda i, at: (0, 0, 0, 0))
    return pl.pallas_call(
        update_kernel,
        grid_spec=pltpu.PrefetchScalarGridSpec(
            num_scalar_prefetch=1,
            grid=(4,),
            in_specs=[
                pl.BlockSpec((tile, cols), lambda i, at: (i, 0)),
                pl.BlockSpec((rows, tile), lambda i, at: (0, i)),
                halves,
                halves,
            ],
            out_specs=pl.BlockSpec((tile, cols), lambda i, at: (i, 0)),
            scratch_shapes=[
                pltpu.VMEM((rows, cols), jnp.float32),
                pltpu.VMEM((rows, cols), jnp.bfloat16),
                pltpu.VMEM((rows, cols), jnp.bfloat16),
            ],
        ),
        out_shape=jax.ShapeDtypeStruct((rows, cols), jnp.float32),
        compiler_params=pltpu.CompilerParams(vmem_limit_bytes=VMEM_LIMIT),
        cost_estimate=pl.CostEstimate(flops=6 * rows * rows * cols, bytes_accessed=10 << 20, transcendentals=0),
    )(at, cotangent, panel, mine, other)


def grad_kernel(at_ref, mine_ref, other_ref, own_ref, left_ref, right_ref, upper_ref, lower_ref, out_ref, high, low):
    i = pl.program_id(0)
    me, q, core = at_ref[0], at_ref[1], at_ref[2]
    half = mine_ref.shape[2]
    quarter = 2 * half
    tile = out_ref.shape[2]
    local_rows = 4 * tile

    @pl.when(i == 0)
    def _():
        for j in range(4):
            for k in range(STEPS):
                a, b = mine_ref[j, k], other_ref[j, k]
                for h in range(2):
                    at = pl.ds((k * 2 + h) * half, half)
                    high[j, at, :], low[j, at, :] = split(-jnp.where(core == h, a, b))

    def term(away, saved):
        j = lax.rem(q + away, NX)
        return dot3((high[j], low[j]), split(saved), LAST)

    total = term(0, own_ref[...]) + term(3, left_ref[...]) + term(1, right_ref[...])
    total += term(2, jnp.where(i < 2, upper_ref[...], lower_ref[...]))
    column = me * local_rows + i * tile + lax.broadcasted_iota(jnp.int32, (quarter, tile), 1)
    row = lax.broadcasted_iota(jnp.int32, (quarter, tile), 0) + q * quarter
    for k in range(STEPS):
        limit = row + (2 * CHIPS * local_rows - (STEPS - k) * 4 * quarter)
        part = total[k * quarter : (k + 1) * quarter]
        out_ref[k] = jnp.where(column <= limit, part, jnp.float32(0.0))


def grad(at, mine, other, own, left, right, upper, lower):
    _, _, half, cols = mine.shape
    rows = own.shape[0]
    tile = rows // 4
    halves = pl.BlockSpec(mine.shape, lambda i, at: (0, 0, 0, 0))
    tiled = pl.BlockSpec((tile, cols), lambda i, at: (i, 0))
    first = pl.BlockSpec((tile, cols), lambda i, at: (jnp.minimum(i, 1), 0))
    last = pl.BlockSpec((tile, cols), lambda i, at: (jnp.maximum(i - 2, 0), 0))
    return pl.pallas_call(
        grad_kernel,
        grid_spec=pltpu.PrefetchScalarGridSpec(
            num_scalar_prefetch=1,
            grid=(4,),
            in_specs=[halves, halves, tiled, tiled, tiled, first, last],
            out_specs=pl.BlockSpec((STEPS, 2 * half, tile), lambda i, at: (0, 0, i)),
            scratch_shapes=[
                pltpu.VMEM((4, STEPS * 2 * half, cols), jnp.bfloat16),
                pltpu.VMEM((4, STEPS * 2 * half, cols), jnp.bfloat16),
            ],
        ),
        out_shape=jax.ShapeDtypeStruct((STEPS, 2 * half, rows), jnp.float32),
        compiler_params=pltpu.CompilerParams(vmem_limit_bytes=VMEM_LIMIT),
        cost_estimate=pl.CostEstimate(flops=96 * half * rows * cols, bytes_accessed=12 << 20, transcendentals=0),
    )(at, mine, other, own, left, right, upper, lower)


def on_device(cotangent, saved, panel, dinv):
    bs = dinv.shape[1]
    local_rows, cols = cotangent.shape
    half = bs // 8
    me = lax.axis_index("rows")
    q = lax.axis_index("cols")
    c = me % 2
    at = jnp.stack([me, q, c]).astype(jnp.int32)

    def swap(x):
        return lax.ppermute(x, "rows", SWAP)

    def right(x):
        return lax.ppermute(x, "cols", X_RIGHT)

    def left(x):
        return lax.ppermute(x, "cols", X_LEFT)

    def scatter(x, groups):
        count = len(groups[0])
        blocks = x.reshape(count, -1, cols)
        return lax.all_to_all(blocks, "rows", 0, 0, axis_index_groups=groups)[count - 1]

    def gather(x, groups):
        count = len(groups[0])
        blocks = jnp.broadcast_to(x[None], (count,) + x.shape)
        return lax.all_to_all(blocks, "rows", 0, 0, axis_index_groups=groups).reshape(-1, cols)

    from_left, from_right = right(saved), left(saved)

    given, kept = solve(cotangent, panel, dinv)
    mine = jnp.where(c == 1, kept.reshape(bs, cols), swap(given.reshape(bs, cols)))
    mine = scatter(scatter(mine, ALONG_Y), ALONG_Z)
    mine = gather(mine, ALONG_Z)
    upper, lower = from_left[: local_rows // 2], from_right[local_rows // 2 :]
    mine, upper, lower = lax.optimization_barrier((mine, upper, lower))
    upper, lower = right(upper), left(lower)
    mine = gather(mine, ALONG_Y)
    mine, other, upper, lower = lax.optimization_barrier((mine, swap(mine), upper, lower))

    wide = lax.all_to_all(mine.reshape(4, STEPS * half, cols), "cols", 0, 0)
    shape = (4, STEPS, half, cols)
    carried = update(at, cotangent, panel, mine.reshape(shape), other.reshape(shape))
    wide, carried = lax.optimization_barrier((wide, carried))
    other = swap(wide.reshape(4 * STEPS * half, cols))
    factor = grad(at, wide.reshape(shape), other.reshape(shape), saved, from_left, from_right, upper, lower)
    return carried, factor


def solution(mesh):
    return jax.shard_map(
        on_device,
        mesh=mesh,
        in_specs=(P("rows", "cols"), P("rows", "cols"), P(None, "rows"), P()),
        out_specs=(P("rows", "cols"), P(None, "cols", "rows")),
        check_vma=False,
    )
```

```python
import jax
import jax.numpy as jnp
from jax import lax
from jax.experimental import pallas as pl
from jax.experimental.pallas import tpu as pltpu
from jax.sharding import PartitionSpec as P

STEPS = 2
LEAD = (((0,), (0,)), ((), ()))
LAST = (((1,), (1,)), ((), ()))
NZ, NY, NX = 8, 4, 4
CHIPS = NZ * NY
ROOT = 2 * CHIPS - 1
VMEM_LIMIT = 60 * 1024 * 1024


def rank(z, y, c):
    return (z * NY + y) * 2 + c


SWAP = [(r, r ^ 1) for r in range(2 * CHIPS)]
ALONG_Y = [[rank(z, y, c) for y in range(NY)] for z in range(NZ) for c in range(2)]
ALONG_Z = [[rank(z, y, c) for z in range(NZ)] for y in range(NY) for c in range(2)]
X_RIGHT = [(q, (q + 1) % NX) for q in range(NX)]
X_LEFT = [(q, (q - 1) % NX) for q in range(NX)]


def split(x):
    high = x.astype(jnp.bfloat16)
    return high, (x - high.astype(jnp.float32)).astype(jnp.bfloat16)


def dot3(a, b, dims):
    def one(x, y):
        return lax.dot_general(x, y, dims, preferred_element_type=jnp.float32)

    return one(a[0], b[0]) + (one(a[0], b[1]) + one(a[1], b[0]))


def solve_kernel(cot_ref, panel_ref, dinv_ref, *out_refs):
    bs = dinv_ref.shape[1]
    half = bs // 8

    def put(k, solved):
        for quarter in range(4):
            for h in range(2):
                row = (quarter * 2 + h) * half
                out_refs[h][quarter, k] = solved[row : row + half]

    solved1 = dot3(split(dinv_ref[1]), split(cot_ref[bs:]), LEAD)
    put(1, solved1)
    left = cot_ref[:bs] - dot3(split(panel_ref[...]), split(solved1), LEAD)
    put(0, dot3(split(dinv_ref[0]), split(left), LEAD))


def solve(cotangent, panel, dinv):
    steps, bs, _ = dinv.shape
    rows, cols = cotangent.shape
    return pl.pallas_call(
        solve_kernel,
        grid=(1,),
        in_specs=[
            pl.BlockSpec((rows, cols), lambda i: (0, 0)),
            pl.BlockSpec((bs, bs), lambda i: (1, 0)),
            pl.BlockSpec((steps, bs, bs), lambda i: (0, 0, 0)),
        ],
        out_specs=[pl.BlockSpec((4, steps, bs // 8, cols), lambda i: (0, 0, 0, 0))] * 2,
        out_shape=[jax.ShapeDtypeStruct((4, steps, bs // 8, cols), jnp.float32)] * 2,
        compiler_params=pltpu.CompilerParams(vmem_limit_bytes=VMEM_LIMIT),
        cost_estimate=pl.CostEstimate(flops=18 * bs * bs * cols, bytes_accessed=7 << 20, transcendentals=0),
    )(cotangent, panel, dinv)


def update_kernel(at_ref, cot_ref, panel_ref, mine_ref, other_ref, out_ref, whole, high, low):
    i = pl.program_id(0)
    half = mine_ref.shape[2]
    tile = out_ref.shape[0]
    core = at_ref[2]

    @pl.when(i == 0)
    def _():
        for k in range(STEPS):
            for quarter in range(4):
                a, b = mine_ref[quarter, k], other_ref[quarter, k]
                for h in range(2):
                    rows = jnp.where(core == h, a, b)
                    at = pl.ds(((k * 4 + quarter) * 2 + h) * half, half)
                    whole[at, :] = rows
                    high[at, :], low[at, :] = split(rows)

    @pl.when(at_ref[0] != ROOT)
    def _():
        product = dot3(split(panel_ref[...]), (high[...], low[...]), LEAD)
        out_ref[...] = cot_ref[...] - product

    @pl.when(at_ref[0] == ROOT)
    def _():
        out_ref[...] = whole[pl.ds(pl.multiple_of(i * tile, tile), tile), :]


def update(at, cotangent, panel, mine, other):
    rows, cols = cotangent.shape
    tile = rows // 4
    halves = pl.BlockSpec(mine.shape, lambda i, at: (0, 0, 0, 0))
    return pl.pallas_call(
        update_kernel,
        grid_spec=pltpu.PrefetchScalarGridSpec(
            num_scalar_prefetch=1,
            grid=(4,),
            in_specs=[
                pl.BlockSpec((tile, cols), lambda i, at: (i, 0)),
                pl.BlockSpec((rows, tile), lambda i, at: (0, i)),
                halves,
                halves,
            ],
            out_specs=pl.BlockSpec((tile, cols), lambda i, at: (i, 0)),
            scratch_shapes=[
                pltpu.VMEM((rows, cols), jnp.float32),
                pltpu.VMEM((rows, cols), jnp.bfloat16),
                pltpu.VMEM((rows, cols), jnp.bfloat16),
            ],
        ),
        out_shape=jax.ShapeDtypeStruct((rows, cols), jnp.float32),
        compiler_params=pltpu.CompilerParams(vmem_limit_bytes=VMEM_LIMIT),
        cost_estimate=pl.CostEstimate(flops=6 * rows * rows * cols, bytes_accessed=10 << 20, transcendentals=0),
    )(at, cotangent, panel, mine, other)


def grad_kernel(at_ref, mine_ref, other_ref, own_ref, left_ref, right_ref, upper_ref, lower_ref, out_ref, high, low):
    i = pl.program_id(0)
    me, q, core = at_ref[0], at_ref[1], at_ref[2]
    half = mine_ref.shape[2]
    quarter = 2 * half
    tile = out_ref.shape[2]
    local_rows = 4 * tile

    @pl.when(i == 0)
    def _():
        for j in range(4):
            for k in range(STEPS):
                a, b = mine_ref[j, k], other_ref[j, k]
                for h in range(2):
                    at = pl.ds((k * 2 + h) * half, half)
                    high[j, at, :], low[j, at, :] = split(-jnp.where(core == h, a, b))

    def term(away, saved):
        j = lax.rem(q + away, NX)
        return dot3((high[j], low[j]), split(saved), LAST)

    total = term(0, own_ref[...]) + term(3, left_ref[...]) + term(1, right_ref[...])
    total += term(2, jnp.where(i < 2, upper_ref[...], lower_ref[...]))
    column = me * local_rows + i * tile + lax.broadcasted_iota(jnp.int32, (quarter, tile), 1)
    row = lax.broadcasted_iota(jnp.int32, (quarter, tile), 0) + q * quarter
    for k in range(STEPS):
        limit = row + (2 * CHIPS * local_rows - (STEPS - k) * 4 * quarter)
        part = total[k * quarter : (k + 1) * quarter]
        out_ref[k] = jnp.where(column <= limit, part, jnp.float32(0.0))


def grad(at, mine, other, own, left, right, upper, lower):
    _, _, half, cols = mine.shape
    rows = own.shape[0]
    tile = rows // 4
    halves = pl.BlockSpec(mine.shape, lambda i, at: (0, 0, 0, 0))
    tiled = pl.BlockSpec((tile, cols), lambda i, at: (i, 0))
    first = pl.BlockSpec((tile, cols), lambda i, at: (jnp.minimum(i, 1), 0))
    last = pl.BlockSpec((tile, cols), lambda i, at: (jnp.maximum(i - 2, 0), 0))
    return pl.pallas_call(
        grad_kernel,
        grid_spec=pltpu.PrefetchScalarGridSpec(
            num_scalar_prefetch=1,
            grid=(4,),
            in_specs=[halves, halves, tiled, tiled, tiled, first, last],
            out_specs=pl.BlockSpec((STEPS, 2 * half, tile), lambda i, at: (0, 0, i)),
            scratch_shapes=[
                pltpu.VMEM((4, STEPS * 2 * half, cols), jnp.bfloat16),
                pltpu.VMEM((4, STEPS * 2 * half, cols), jnp.bfloat16),
            ],
        ),
        out_shape=jax.ShapeDtypeStruct((STEPS, 2 * half, rows), jnp.float32),
        compiler_params=pltpu.CompilerParams(vmem_limit_bytes=VMEM_LIMIT),
        cost_estimate=pl.CostEstimate(flops=96 * half * rows * cols, bytes_accessed=12 << 20, transcendentals=0),
    )(at, mine, other, own, left, right, upper, lower)


def on_device(cotangent, saved, panel, dinv):
    bs = dinv.shape[1]
    local_rows, cols = cotangent.shape
    half = bs // 8
    me = lax.axis_index("rows")
    q = lax.axis_index("cols")
    c = me % 2
    at = jnp.stack([me, q, c]).astype(jnp.int32)

    def swap(x):
        return lax.ppermute(x, "rows", SWAP)

    def right(x):
        return lax.ppermute(x, "cols", X_RIGHT)

    def left(x):
        return lax.ppermute(x, "cols", X_LEFT)

    def scatter(x, groups):
        count = len(groups[0])
        blocks = x.reshape(count, -1, cols)
        return lax.all_to_all(blocks, "rows", 0, 0, axis_index_groups=groups)[count - 1]

    def gather(x, groups):
        count = len(groups[0])
        blocks = jnp.broadcast_to(x[None], (count,) + x.shape)
        return lax.all_to_all(blocks, "rows", 0, 0, axis_index_groups=groups).reshape(-1, cols)

    from_left, from_right = right(saved), left(saved)

    given, kept = solve(cotangent, panel, dinv)
    mine = jnp.where(c == 1, kept.reshape(bs, cols), swap(given.reshape(bs, cols)))
    mine = scatter(scatter(mine, ALONG_Y), ALONG_Z)
    mine = gather(mine, ALONG_Z)
    upper, lower = right(from_left[: local_rows // 2]), left(from_right[local_rows // 2 :])
    mine = gather(mine, ALONG_Y)
    mine, upper, lower = lax.optimization_barrier((mine, upper, lower))
    other = swap(mine)

    wide = lax.all_to_all(mine.reshape(4, STEPS * half, cols), "cols", 0, 0)
    shape = (4, STEPS, half, cols)
    carried = update(at, cotangent, panel, mine.reshape(shape), other.reshape(shape))
    wide, carried = lax.optimization_barrier((wide, carried))
    other = swap(wide.reshape(4 * STEPS * half, cols))
    factor = grad(at, wide.reshape(shape), other.reshape(shape), saved, from_left, from_right, upper, lower)
    return carried, factor


def solution(mesh):
    return jax.shard_map(
        on_device,
        mesh=mesh,
        in_specs=(P("rows", "cols"), P("rows", "cols"), P(None, "rows"), P()),
        out_specs=(P("rows", "cols"), P(None, "cols", "rows")),
        check_vma=False,
    )
```

```python
import jax
import jax.numpy as jnp
from jax import lax
from jax.experimental import pallas as pl
from jax.experimental.pallas import tpu as pltpu
from jax.sharding import PartitionSpec as P

STEPS = 2
LEAD = (((0,), (0,)), ((), ()))
LAST = (((1,), (1,)), ((), ()))
NZ, NY, NX = 8, 4, 4
CHIPS = NZ * NY
ROOT = 2 * CHIPS - 1
VMEM_LIMIT = 60 * 1024 * 1024


def rank(z, y, c):
    return (z * NY + y) * 2 + c


SWAP = [(r, r ^ 1) for r in range(2 * CHIPS)]
ALONG_Y = [[rank(z, y, c) for y in range(NY)] for z in range(NZ) for c in range(2)]
ALONG_Z = [[rank(z, y, c) for z in range(NZ)] for y in range(NY) for c in range(2)]
X_RIGHT = [(q, (q + 1) % NX) for q in range(NX)]
X_LEFT = [(q, (q - 1) % NX) for q in range(NX)]
X_ACROSS = [(q, (q + 2) % NX) for q in range(NX)]


def split(x):
    high = x.astype(jnp.bfloat16)
    return high, (x - high.astype(jnp.float32)).astype(jnp.bfloat16)


def dot3(a, b, dims):
    def one(x, y):
        return lax.dot_general(x, y, dims, preferred_element_type=jnp.float32)

    return one(a[0], b[0]) + (one(a[0], b[1]) + one(a[1], b[0]))


def solve_kernel(cot_ref, panel_ref, dinv_ref, *out_refs):
    bs = dinv_ref.shape[1]
    half = bs // 8

    def put(k, solved):
        for quarter in range(4):
            for h in range(2):
                row = (quarter * 2 + h) * half
                out_refs[h][quarter, k] = solved[row : row + half]

    solved1 = dot3(split(dinv_ref[1]), split(cot_ref[bs:]), LEAD)
    put(1, solved1)
    left = cot_ref[:bs] - dot3(split(panel_ref[...]), split(solved1), LEAD)
    put(0, dot3(split(dinv_ref[0]), split(left), LEAD))


def solve(cotangent, panel, dinv):
    steps, bs, _ = dinv.shape
    rows, cols = cotangent.shape
    return pl.pallas_call(
        solve_kernel,
        grid=(1,),
        in_specs=[
            pl.BlockSpec((rows, cols), lambda i: (0, 0)),
            pl.BlockSpec((bs, bs), lambda i: (1, 0)),
            pl.BlockSpec((steps, bs, bs), lambda i: (0, 0, 0)),
        ],
        out_specs=[pl.BlockSpec((4, steps, bs // 8, cols), lambda i: (0, 0, 0, 0))] * 2,
        out_shape=[jax.ShapeDtypeStruct((4, steps, bs // 8, cols), jnp.float32)] * 2,
        compiler_params=pltpu.CompilerParams(vmem_limit_bytes=VMEM_LIMIT),
        cost_estimate=pl.CostEstimate(flops=18 * bs * bs * cols, bytes_accessed=7 << 20, transcendentals=0),
    )(cotangent, panel, dinv)


def update_kernel(at_ref, cot_ref, panel_ref, mine_ref, other_ref, out_ref, whole, high, low):
    i = pl.program_id(0)
    half = mine_ref.shape[2]
    tile = out_ref.shape[0]
    core = at_ref[2]

    @pl.when(i == 0)
    def _():
        for k in range(STEPS):
            for quarter in range(4):
                a, b = mine_ref[quarter, k], other_ref[quarter, k]
                for h in range(2):
                    rows = jnp.where(core == h, a, b)
                    at = pl.ds(((k * 4 + quarter) * 2 + h) * half, half)
                    whole[at, :] = rows
                    high[at, :], low[at, :] = split(rows)

    @pl.when(at_ref[0] != ROOT)
    def _():
        product = dot3(split(panel_ref[...]), (high[...], low[...]), LEAD)
        out_ref[...] = cot_ref[...] - product

    @pl.when(at_ref[0] == ROOT)
    def _():
        out_ref[...] = whole[pl.ds(pl.multiple_of(i * tile, tile), tile), :]


def update(at, cotangent, panel, mine, other):
    rows, cols = cotangent.shape
    tile = rows // 4
    halves = pl.BlockSpec(mine.shape, lambda i, at: (0, 0, 0, 0))
    return pl.pallas_call(
        update_kernel,
        grid_spec=pltpu.PrefetchScalarGridSpec(
            num_scalar_prefetch=1,
            grid=(4,),
            in_specs=[
                pl.BlockSpec((tile, cols), lambda i, at: (i, 0)),
                pl.BlockSpec((rows, tile), lambda i, at: (0, i)),
                halves,
                halves,
            ],
            out_specs=pl.BlockSpec((tile, cols), lambda i, at: (i, 0)),
            scratch_shapes=[
                pltpu.VMEM((rows, cols), jnp.float32),
                pltpu.VMEM((rows, cols), jnp.bfloat16),
                pltpu.VMEM((rows, cols), jnp.bfloat16),
            ],
        ),
        out_shape=jax.ShapeDtypeStruct((rows, cols), jnp.float32),
        compiler_params=pltpu.CompilerParams(vmem_limit_bytes=VMEM_LIMIT),
        cost_estimate=pl.CostEstimate(flops=6 * rows * rows * cols, bytes_accessed=10 << 20, transcendentals=0),
    )(at, cotangent, panel, mine, other)


def grad_kernel(at_ref, *refs):
    pairs, saved_refs, (out_ref, high, low) = refs[:8], refs[8:13], refs[13:]
    own_ref, left_ref, right_ref, upper_ref, lower_ref = saved_refs
    i = pl.program_id(0)
    me, q, core = at_ref[0], at_ref[1], at_ref[2]
    half = pairs[0].shape[2]
    quarter = 2 * half
    tile = out_ref.shape[2]
    local_rows = 2 * tile

    @pl.when(i == 0)
    def _():
        for j in range(4):
            for k in range(STEPS):
                a, b = pairs[2 * j][0, k], pairs[2 * j + 1][0, k]
                for h in range(2):
                    at = pl.ds((k * 2 + h) * half, half)
                    high[j, at, :], low[j, at, :] = split(-jnp.where(core == h, a, b))

    def term(j, saved):
        return dot3((high[j], low[j]), split(saved), LAST)

    total = term(0, own_ref[...]) + term(1, left_ref[...]) + term(2, right_ref[...])
    total += term(3, jnp.where(i == 0, upper_ref[...], lower_ref[...]))
    column = me * local_rows + i * tile + lax.broadcasted_iota(jnp.int32, (quarter, tile), 1)
    row = lax.broadcasted_iota(jnp.int32, (quarter, tile), 0) + q * quarter
    for k in range(STEPS):
        limit = row + (2 * CHIPS * local_rows - (STEPS - k) * 4 * quarter)
        part = total[k * quarter : (k + 1) * quarter]
        out_ref[k] = jnp.where(column <= limit, part, jnp.float32(0.0))


def grad(at, mine, other, near, own, left, right, upper, lower):
    _, _, half, cols = mine.shape
    rows = own.shape[0]
    tile = rows // 2
    mine_part = pl.BlockSpec((1, STEPS, half, cols), lambda i, at: (at[1], 0, 0, 0))
    near_part = pl.BlockSpec((1, STEPS, half, cols), lambda i, at: (0, 0, 0, 0))
    tiled = pl.BlockSpec((tile, cols), lambda i, at: (i, 0))
    fixed = pl.BlockSpec((tile, cols), lambda i, at: (0, 0))
    return pl.pallas_call(
        grad_kernel,
        grid_spec=pltpu.PrefetchScalarGridSpec(
            num_scalar_prefetch=1,
            grid=(2,),
            in_specs=[mine_part] * 2 + [near_part] * 6 + [tiled] * 3 + [fixed] * 2,
            out_specs=pl.BlockSpec((STEPS, 2 * half, tile), lambda i, at: (0, 0, i)),
            scratch_shapes=[pltpu.VMEM((4, STEPS * 2 * half, cols), jnp.bfloat16)] * 2,
        ),
        out_shape=jax.ShapeDtypeStruct((STEPS, 2 * half, rows), jnp.float32),
        compiler_params=pltpu.CompilerParams(vmem_limit_bytes=VMEM_LIMIT),
        cost_estimate=pl.CostEstimate(flops=96 * half * rows * cols, bytes_accessed=12 << 20, transcendentals=0),
    )(at, mine, other, *near, own, left, right, upper, lower)


def on_device(cotangent, saved, panel, dinv):
    bs = dinv.shape[1]
    local_rows, cols = cotangent.shape
    half = bs // 8
    me = lax.axis_index("rows")
    q = lax.axis_index("cols")
    c = me % 2
    at = jnp.stack([me, q, c]).astype(jnp.int32)

    def swap(x):
        return lax.ppermute(x, "rows", SWAP)

    def right(x):
        return lax.ppermute(x, "cols", X_RIGHT)

    def left(x):
        return lax.ppermute(x, "cols", X_LEFT)

    def scatter(x, groups):
        count = len(groups[0])
        blocks = x.reshape(count, -1, cols)
        return lax.all_to_all(blocks, "rows", 0, 0, axis_index_groups=groups)[count - 1]

    def gather(x, groups):
        count = len(groups[0])
        blocks = jnp.broadcast_to(x[None], (count,) + x.shape)
        return lax.all_to_all(blocks, "rows", 0, 0, axis_index_groups=groups).reshape(-1, cols)

    from_left, from_right = right(saved), left(saved)

    given, kept = solve(cotangent, panel, dinv)
    mine = jnp.where(c == 1, kept.reshape(bs, cols), swap(given.reshape(bs, cols)))
    mine = scatter(scatter(mine, ALONG_Y), ALONG_Z)
    mine = gather(mine, ALONG_Z)
    upper, lower = right(from_left[: local_rows // 2]), left(from_right[local_rows // 2 :])
    mine = gather(mine, ALONG_Y)
    mine, upper, lower = lax.optimization_barrier((mine, upper, lower))
    other = swap(mine)

    def of_quarter(away):
        n = STEPS * half
        return lax.dynamic_slice_in_dim(mine, lax.rem(q + away, NX) * n, n, 0)

    near = [right(of_quarter(1)), left(of_quarter(3)), lax.ppermute(of_quarter(2), "cols", X_ACROSS)]
    shape = (4, STEPS, half, cols)
    carried = update(at, cotangent, panel, mine.reshape(shape), other.reshape(shape))
    near, carried = lax.optimization_barrier((near, carried))
    near = [part.reshape(1, STEPS, half, cols) for rows in near for part in (rows, swap(rows))]
    factor = grad(at, mine.reshape(shape), other.reshape(shape), near, saved, from_left, from_right, upper, lower)
    return carried, factor


def solution(mesh):
    return jax.shard_map(
        on_device,
        mesh=mesh,
        in_specs=(P("rows", "cols"), P("rows", "cols"), P(None, "rows"), P()),
        out_specs=(P("rows", "cols"), P(None, "cols", "rows")),
        check_vma=False,
    )
```
